32 devices in a mesh: inst: 16 (over z, x, core), tp: 2 (over y).
Axes of the slice: x: 2, y: 2, z: 4, core: 2. Of those that a mesh axis runs over, the one named last changes fastest.
Arguments:
- queries: bfloat16 [2, 4, 192, 8192], P(None, None, 'inst', 'tp'), may hold values from -125 to 125
- cache_keys: bfloat16 [2, 192, 128, 1024], P(None, 'inst', None, 'tp'), may hold values from -4.5 to 4.5
- cache_values: bfloat16 [2, 192, 128, 1024], P(None, 'inst', None, 'tp'), may hold values from -6 to 6
- new_keys: bfloat16 [2, 4, 192, 1024], P(None, None, 'inst', 'tp'), may hold values from -8 to 8
- new_values: bfloat16 [2, 4, 192, 1024], P(None, None, 'inst', 'tp'), may hold values from -6 to 6
- kv_pool: bfloat16 [1280, 2, 2, 16, 1024], P('inst', None, None, None, 'tp'), may hold values from -6 to 6
- mig_lengths: int32 [16], replicated, may hold values from 256 to 1024, as said below
- mig_source: int32 [16], replicated, may hold values from 0 to 15, as said below
- mig_target: int32 [16], replicated, may hold values from 0 to 15, as said below
- block_lists: int32 [16, 64], replicated, may hold values from 0 to 79, as said below
- owner_map: int32 [16, 64], replicated, may hold values from 0 to 31
- check_key: bfloat16 [2, 2, 1024, 128], P(None, None, 'tp'), may hold values from -0.5 to 0.5
Outputs:
- attention: bfloat16 [2, 4, 192, 8192], P(None, None, 'inst', 'tp')
- arrived: bfloat16 [1024, 2, 2, 16, 1024], P('inst', None, None, None, 'tp')
- checksums: float32 [32, 128], P('inst')
The draws below stay inside these ranges and needn't reach their ends.
Inputs may be any that keep to these rules, and one draw needn't show every extreme that they name: `mig_lengths`: some request has exactly 1024 tokens and some exactly 256. `mig_source`: each instance drains exactly one request. `mig_target`: each instance receives exactly one request, never its own. `block_lists`: the slots of one row are distinct.
All inputs are finite; a program needn't handle non-finite values.
Results may differ from the reference program's by a relative error of at most 0.015.
Values may be sent and summed in bfloat16 or wider, within the bound.
A program may use at most 64 MiB of HBM per device.

```python
import math
import jax
import jax.numpy as jnp
from jax import lax

QH = 64
KVH = 8
HD = 128
CSUM = 128
LAYERS = 2
STEPS = 4
BLOCK = 16
MAXBLK = 64
REQ_DEC = 12
CTX = 128
QW = 8192
KW = 1024
REQS = 192
MIGS = 16
POOL = 80
MAXLEN = 1024
CHECKS = 32
N_INST = 16


def pair_order(key):
    first = jax.random.permutation(jax.random.fold_in(key, 11), MIGS).astype(jnp.int32)
    cycle = jax.random.permutation(jax.random.fold_in(key, 12), MIGS).astype(jnp.int32)
    following = jnp.zeros((MIGS,), jnp.int32).at[cycle].set(jnp.roll(cycle, -1))
    return (first, following[first])


def key_field(key):
    base = jax.random.normal(jax.random.fold_in(key, 21), (LAYERS, REQS, CTX, KW), jnp.float32)
    return jnp.clip(base, -4.0, 4.0)


def draw_mig_source(key, part):
    return pair_order(key)[0]


def draw_mig_target(key, part):
    return pair_order(key)[1]


def draw_mig_lengths(key, part):
    key = jax.random.fold_in(key, 3)
    lengths = jax.random.randint(key, (MIGS,), MAXLEN // 4, MAXLEN + 1).astype(jnp.int32)
    chosen = jax.random.randint(jax.random.fold_in(key, 4), (), 0, MIGS)
    order = jnp.arange(MIGS, dtype=jnp.int32)
    lengths = jnp.where(order == chosen, MAXLEN, lengths)
    lengths = jnp.where(order == (chosen + 1) % MIGS, MAXLEN // 4, lengths)
    return lengths.astype(jnp.int32)


def draw_block_lists(key, part):
    key = jax.random.fold_in(key, 5)
    keys = jax.random.split(key, MIGS)
    rows = jax.vmap(lambda single: jax.random.permutation(single, POOL)[:MAXBLK])(keys)
    return rows.astype(jnp.int32)


def draw_cache_keys(key, part):
    base = key_field(key)
    return base.astype(jnp.bfloat16)


def draw_queries(key, part):
    key = jax.random.fold_in(key, 7)
    fresh = jnp.clip(jax.random.normal(key, (LAYERS, STEPS, REQS, QW), jnp.float32), -4.0, 4.0)
    return fresh.astype(jnp.bfloat16)


def place_ends(array, stream_key, least, largest):
    spot = [jax.random.randint(jax.random.fold_in(stream_key, axis), (), 0, length) for axis, length in enumerate(array.shape)]
    main_axis = array.shape.index(max(array.shape))
    next_to = spot[:main_axis] + [(spot[main_axis] + 1) % array.shape[main_axis]] + spot[main_axis + 1:]
    return array.at[tuple(spot)].set(least).at[tuple(next_to)].set(largest)


def steps_of(stream_key, extent, shards, low, largest):
    factor_of, own = 1.0, jax.random.fold_in(stream_key, 6)
    for dim, parts in shards:
        steps = jnp.exp(jax.random.uniform(jax.random.fold_in(own, dim), (parts,), jnp.float32, low / len(shards), largest / len(shards)))
        factor_of = factor_of * jnp.repeat(steps, extent[dim] // parts).reshape([-1 if axis == dim else 1 for axis in range(len(extent))])
    return factor_of


def scatter_about(key, extent, scale, bound, cuts=(), kind=jnp.bfloat16):
    array = scale * jax.random.normal(key, extent, jnp.float32)
    if cuts:
        array = array * steps_of(key, extent, cuts, -0.22, 0.18)
    return jnp.clip(array, -bound, bound).astype(kind)


def setup_inputs(seed: int = 0) -> dict:
    arg_keys = jax.random.split(jax.random.key(seed), 13)
    return {
        "queries": draw_queries(jax.random.fold_in(arg_keys[12], 71), 0),
        "cache_keys": draw_cache_keys(jax.random.fold_in(arg_keys[12], 71), 0),
        "cache_values": scatter_about(arg_keys[2], (LAYERS, REQS, CTX, KW), 1.0, 6.0, ((1, 16), (3, 2))),
        "new_keys": scatter_about(arg_keys[3], (LAYERS, STEPS, REQS, KW), 2.0, 8.0, ((2, 16), (3, 2))),
        "new_values": scatter_about(arg_keys[4], (LAYERS, STEPS, REQS, KW), 1.0, 6.0, ((2, 16), (3, 2))),
        "kv_pool": scatter_about(arg_keys[5], (MIGS * POOL, LAYERS, 2, BLOCK, KW), 1.0, 6.0, ((0, 16), (4, 2))),
        "mig_lengths": draw_mig_lengths(jax.random.fold_in(arg_keys[12], 71), 0),
        "mig_source": draw_mig_source(jax.random.fold_in(arg_keys[12], 71), 0),
        "mig_target": draw_mig_target(jax.random.fold_in(arg_keys[12], 71), 0),
        "block_lists": draw_block_lists(jax.random.fold_in(arg_keys[12], 71), 0),
        "owner_map": place_ends(jax.random.randint(arg_keys[10], (MIGS, MAXBLK), 0, CHECKS), jax.random.fold_in(arg_keys[10], 1), 0, CHECKS - 1).astype(jnp.int32),
        "check_key": scatter_about(arg_keys[11], (LAYERS, 2, KW, CSUM), HD ** -0.5, 0.5, ((2, 2),)),
    }


def attend_group(inputs):
    query, keyed, valued, fresh_keys, fresh_values = inputs
    group = QH // KVH
    rows = query.shape[2]
    query = query.astype(jnp.float32).reshape(LAYERS, STEPS, rows, KVH, group, HD)
    keyed = keyed.astype(jnp.float32).reshape(LAYERS, rows, CTX, KVH, HD)
    valued = valued.astype(jnp.float32).reshape(LAYERS, rows, CTX, KVH, HD)
    fresh_keys = fresh_keys.astype(jnp.float32).reshape(LAYERS, STEPS, rows, KVH, HD)
    fresh_values = fresh_values.astype(jnp.float32).reshape(LAYERS, STEPS, rows, KVH, HD)
    layer_outs = []
    for layer in range(LAYERS):
        step_outs = []
        for step in range(STEPS):
            all_keys = jnp.concatenate([keyed[layer], jnp.moveaxis(fresh_keys[layer, :step + 1], 0, 1)], axis=1)
            all_values = jnp.concatenate([valued[layer], jnp.moveaxis(fresh_values[layer, :step + 1], 0, 1)], axis=1)
            scores = jnp.einsum('rkgd,rckd->rkgc', query[layer, step], all_keys) / math.sqrt(HD)
            highest = lax.optimization_barrier(jnp.max(scores, axis=-1, keepdims=True))
            expd = jnp.exp(scores - highest)
            weights = (expd / lax.optimization_barrier(jnp.sum(expd, axis=-1, keepdims=True))).astype(jnp.bfloat16)
            weights = lax.optimization_barrier(weights).astype(jnp.float32)
            mixed = jnp.einsum('rkgc,rckd->rkgd', weights, all_values)
            step_outs.append(mixed.astype(jnp.bfloat16).reshape(rows, QW))
        layer_outs.append(jnp.stack(step_outs))
    return jnp.stack(layer_outs)

def reference(queries, cache_keys, cache_values, new_keys, new_values, kv_pool, mig_lengths, mig_source, mig_target, block_lists, owner_map, check_key):
    grouped = (queries.reshape(LAYERS, STEPS, N_INST, REQ_DEC, QW).transpose(2, 0, 1, 3, 4), cache_keys.reshape(LAYERS, N_INST, REQ_DEC, CTX, KW).transpose(1, 0, 2, 3, 4), cache_values.reshape(LAYERS, N_INST, REQ_DEC, CTX, KW).transpose(1, 0, 2, 3, 4), new_keys.reshape(LAYERS, STEPS, N_INST, REQ_DEC, KW).transpose(2, 0, 1, 3, 4), new_values.reshape(LAYERS, STEPS, N_INST, REQ_DEC, KW).transpose(2, 0, 1, 3, 4))
    attended = lax.map(attend_group, grouped)
    attention = attended.transpose(1, 2, 0, 3, 4).reshape(LAYERS, STEPS, REQS, QW)
    rows = (mig_source[:, None] * POOL + block_lists).astype(jnp.int32)
    taken = kv_pool[rows]
    position = jnp.arange(MAXBLK, dtype=jnp.int32)[:, None] * BLOCK + jnp.arange(BLOCK, dtype=jnp.int32)[None, :]
    live = position[None, :, :] < mig_lengths[:, None, None]
    taken = jnp.where(live[:, :, None, None, :, None], taken, jnp.zeros((), kv_pool.dtype))
    arrived = jnp.zeros_like(taken).at[mig_target].set(taken)
    arrived = arrived.reshape(MIGS * MAXBLK, LAYERS, 2, BLOCK, KW)
    projection = check_key.astype(jnp.float32).reshape(LAYERS, 2, KVH, HD, CSUM)

    def digest_one(request_blocks):
        grid = request_blocks.astype(jnp.float32).reshape(MAXBLK, LAYERS, 2, BLOCK, KVH, HD)
        projected = jnp.einsum('blktgd,lkgde->blktge', grid, projection, precision=lax.Precision.HIGHEST)
        return lax.optimization_barrier(jnp.sum(jnp.tanh(projected), axis=(1, 2, 3, 4))) / 16.0
    digest = lax.map(digest_one, taken)
    checksums = jnp.zeros((CHECKS, CSUM), jnp.float32).at[owner_map.reshape(-1)].add(digest.reshape(-1, CSUM))
    return (attention, arrived, checksums)
```

```python
import functools
import math

import jax
import jax.numpy as jnp
from jax import lax
from jax.experimental import pallas as pl
from jax.experimental.pallas import tpu as pltpu
from jax.sharding import PartitionSpec as P

HD = 128
SLOTS = 2
LAG = 6
ROUNDS = (96, 120, 144, 176, 256)
RMAX = ROUNDS[-1]
VMEM_LIMIT = 60 * 1024 * 1024
MESH = pl.DeviceIdType.MESH


def plan_kernel(
    members,
    len_ref,
    src_ref,
    tgt_ref,
    list_ref,
    pool_ref,
    key_ref,
    table_ref,
    info_ref,
    staged_ref,
    digest_ref,
    free,
    done,
    sem,
):
    me = lax.axis_index("inst")
    requests = len_ref.shape[0]
    depth = list_ref.shape[1]
    span = staged_ref.shape[2] // 2
    chip = me // 2
    rows = members // 4

    def find(r, found):
        return jnp.where(src_ref[r] == me, r, found)

    own = lax.fori_loop(0, requests, find, jnp.int32(0))

    def fetch(b, _):
        pltpu.make_async_copy(pool_ref.at[list_ref[own, b]], staged_ref.at[:, b], sem).start()
        return 0

    lax.fori_loop(0, depth, fetch, 0)

    def clear(i, _):
        table_ref[i] = 0
        return 0

    lax.fori_loop(0, table_ref.shape[0], clear, 0)

    def clear_free(i, _):
        free[i] = 0
        return 0

    lax.fori_loop(0, free.shape[0], clear_free, 0)

    def clear_done(i, _):
        done[i] = 0
        return 0

    lax.fori_loop(0, requests, clear_done, 0)
    for i in range(8):
        info_ref[i] = 0

    def schedule(_, longest):
        def pick(r, best):
            score = jnp.where(done[r] == 0, len_ref[r], 0)
            better = score > best[0]
            return jnp.where(better, score, best[0]), jnp.where(better, r, best[1])

        tokens, r = lax.fori_loop(0, requests, pick, (jnp.int32(0), jnp.int32(0)))
        done[r] = 1
        count = (tokens + span - 1) // span
        source, target = src_ref[r], tgt_ref[r]
        from_row, from_col = source // 4, (source // 2) % 2
        to_row, to_col = target // 4, (target // 2) % 2
        cross = from_col != to_col
        up = to_row > from_row
        hops = jnp.abs(to_row - from_row)
        step = jnp.where(up, 1, -1)
        port = jnp.where(up, 0, 1)

        def slot(link, ready):
            return jnp.maximum(ready, free[link])

        def zlink(col, row):
            return (port * 2 + col) * rows + row

        def xlink(row):
            return (4 + from_col) * rows + row

        def run(col, ready):
            def hop(i, state):
                ready, _ = state
                begin = slot(zlink(col, from_row + i * step), ready)
                return begin + LAG, begin

            return lax.fori_loop(0, hops, hop, (ready, ready))

        ready, last = run(from_col, jnp.int32(0))
        z_first = jnp.where(cross, slot(xlink(to_row), ready), last)
        begin = slot(xlink(from_row), jnp.int32(0))
        ready, last = run(to_col, begin + LAG)
        x_first = jnp.where(hops > 0, last, begin)
        x_leads = jnp.logical_and(cross, x_first < z_first)

        first_base = jnp.where(source == me, 0, depth)

        def take(link, sender, way, ready, base):
            begin = slot(link, ready)
            free[link] = begin + count

            @pl.when(jnp.logical_and(sender == chip, begin + count <= RMAX))
            def _():
                def fill(i, _):
                    table_ref[way * RMAX + begin + i] = base + i
                    return 0

                lax.fori_loop(0, count, fill, 0)

            return (
                begin + LAG,
                2 * depth + way * RMAX + begin,
                jnp.maximum(begin + count, 0),
            )

        def x_move(row, state):
            return lax.cond(
                cross,
                lambda s: take(xlink(row), row * 2 + from_col, 2, s[0], s[1]),
                lambda s: s,
                state,
            )

        def z_move(col, state):
            def hop(i, s):
                row = from_row + i * step
                return take(zlink(col, row), row * 2 + col, port, s[0], s[1])

            return lax.fori_loop(0, hops, hop, state)

        state = (jnp.int32(0), first_base, jnp.int32(0))
        state = lax.cond(
            x_leads,
            lambda s: z_move(to_col, x_move(from_row, s)),
            lambda s: x_move(to_row, z_move(from_col, s)),
            state,
        )
        _, base, end = state

        @pl.when(target == me)
        def _():
            info_ref[0] = base
            info_ref[1] = count

        @pl.when(jnp.logical_and(target // 2 == chip, target != me))
        def _():
            info_ref[2] = base
            info_ref[3] = count

        return jnp.maximum(longest, end)

    longest = lax.fori_loop(0, requests, schedule, jnp.int32(0))
    choice = jnp.int32(0)
    for size in ROUNDS:
        choice = choice + jnp.where(longest > size, 1, 0)
    info_ref[4] = choice
    info_ref[5] = longest

    pltpu.make_async_copy(staged_ref, staged_ref, sem).wait()
    length = len_ref[own]

    def mask(b, _):
        block = staged_ref[:, b]
        token = lax.rem(lax.broadcasted_iota(jnp.int32, block.shape, 1), span) + b * span
        staged_ref[:, b] = jnp.where(token < length, block, jnp.zeros_like(block))
        return 0

    lax.fori_loop(length // span, depth, mask, 0)

    group = 16
    heads = staged_ref.shape[3] // HD
    layers = staged_ref.shape[0]

    def digest(i, _):
        total = jnp.zeros((group * span, key_ref.shape[-1]), jnp.float32)
        at = pl.ds(pl.multiple_of(i * group, group), group)
        for layer in range(layers):
            for kind in range(2):
                for head in range(heads):
                    lanes = pl.ds(head * HD, HD)
                    part = staged_ref[layer, at, pl.ds(kind * span, span), lanes]
                    projected = jnp.dot(
                        part.reshape(group * span, HD),
                        key_ref[layer, kind, lanes, :],
                        preferred_element_type=jnp.float32,
                    )
                    total = total + jnp.tanh(projected)
        digest_ref[at, :] = jnp.sum(total.reshape(group, span, -1), axis=1) * (1.0 / 16.0)
        return 0

    lax.fori_loop(0, depth // group, digest, 0)


def plan(lengths, source, target, lists, pool, check_key, members):
    depth = lists.shape[1]
    layers, width = pool.shape[1], pool.shape[3]
    smem = pl.BlockSpec(memory_space=pltpu.SMEM)
    vmem = pl.BlockSpec(memory_space=pltpu.VMEM)
    return pl.pallas_call(
        functools.partial(plan_kernel, members),
        out_shape=(
            jax.ShapeDtypeStruct((3 * RMAX,), jnp.int32),
            jax.ShapeDtypeStruct((8,), jnp.int32),
            jax.ShapeDtypeStruct((layers, depth, pool.shape[2], width), pool.dtype),
            jax.ShapeDtypeStruct((depth, check_key.shape[-1]), jnp.float32),
        ),
        in_specs=[smem, smem, smem, smem, pl.BlockSpec(memory_space=pl.ANY), vmem],
        out_specs=(smem, smem, vmem, vmem),
        scratch_shapes=[
            pltpu.SMEM((6 * (members // 4),), jnp.int32),
            pltpu.SMEM((lengths.shape[0],), jnp.int32),
            pltpu.SemaphoreType.DMA,
        ],
        compiler_params=pltpu.CompilerParams(vmem_limit_bytes=VMEM_LIMIT),
        name="plan_and_digest",
    )(lengths, source, target, lists, pool, check_key)


def route_kernel(
    rounds,
    members,
    groups,
    table_ref,
    info_ref,
    staged_ref,
    terms_ref,
    out_ref,
    sums_ref,
    store,
    stage,
    ring,
    theirs,
    mine,
    landed,
    shared,
    swap_sems,
    stage_sems,
    ring_sems,
    term_send,
    term_recv,
    share_send,
    share_recv,
):
    me = lax.axis_index("inst")
    group = lax.axis_index("tp")
    core, row = me % 2, me // 4
    depth = staged_ref.shape[1]
    zero = store.shape[0] - 1
    partner = me + 1 - 2 * core
    beside = me + 2 - 4 * ((me // 2) % 2)
    has_up = row < members // 4 - 1
    has_down = row > 0
    ways = (
        (0, me + 4, has_up, has_down),
        (1, me - 4, has_down, has_up),
        (2, beside, None, None),
    )

    def when(condition, body):
        if condition is None:
            body()
        else:
            pl.when(condition)(body)

    barrier = pltpu.get_barrier_semaphore()

    def greet(k, _):
        pl.semaphore_signal(
            barrier, inc=1, device_id={"inst": lax.rem(me + k, members)}, device_id_type=MESH
        )
        return 0

    def greet_group(k, _):
        pl.semaphore_signal(
            barrier, inc=1, device_id={"tp": lax.rem(group + k, groups)}, device_id_type=MESH
        )
        return 0

    lax.fori_loop(1, members, greet, 0)
    lax.fori_loop(1, groups, greet_group, 0)
    pl.semaphore_wait(barrier, members + groups - 2)

    swap = pltpu.make_async_remote_copy(
        src_ref=staged_ref.at[1 - core],
        dst_ref=store.at[pl.ds(depth, depth)],
        send_sem=swap_sems.at[0],
        recv_sem=swap_sems.at[1],
        device_id={"inst": partner},
        device_id_type=MESH,
    )
    swap.start()

    def term(k):
        other = lax.rem(me + k, members)
        return pltpu.make_async_remote_copy(
            src_ref=terms_ref.at[other],
            dst_ref=landed.at[me],
            send_sem=term_send.at[other],
            recv_sem=term_recv.at[me],
            device_id={"inst": other},
            device_id_type=MESH,
        )

    def send_term(k, _):
        term(k).start()
        return 0

    lax.fori_loop(1, members, send_term, 0)

    def keep(b, _):
        store[b] = staged_ref[core, b]
        return 0

    lax.fori_loop(0, depth, keep, 0)
    store[zero] = jnp.zeros(store.shape[1:], store.dtype)
    landed[me] = terms_ref[me]
    swap.wait()

    def hand(way, to, t):
        return pltpu.make_async_remote_copy(
            src_ref=stage.at[way, lax.rem(t, LAG)],
            dst_ref=ring.at[way, lax.rem(t, 2 * LAG)],
            send_sem=stage_sems.at[way, lax.rem(t, LAG)],
            recv_sem=ring_sems.at[way, lax.rem(t, 2 * LAG)],
            device_id={"inst": to},
            device_id_type=MESH,
        )

    def receive(t):
        for way, to, sends, receives in ways:

            def body(way=way, to=to):
                hand(way, to, t).wait_recv()
                store[2 * depth + way * RMAX + t] = ring[way, lax.rem(t, 2 * LAG)]

            when(receives, body)

    def release(t):
        for way, to, sends, receives in ways:

            def body(way=way, to=to):
                hand(way, to, t).wait_send()

            when(sends, body)

    def send(t):
        for way, to, sends, receives in ways:

            def body(way=way, to=to):
                stage[way, lax.rem(t, LAG)] = store[table_ref[way * RMAX + t]]
                hand(way, to, t).start()

            when(sends, body)

    def opening(t, _):
        send(t)
        return 0

    def steady(t, _):
        receive(t - LAG)
        release(t - LAG)
        send(t)
        return 0

    def closing(t, _):
        receive(t - LAG)
        release(t - LAG)
        return 0

    lax.fori_loop(0, LAG, opening, 0)

    def take_term(k, _):
        other = lax.rem(me + k, members)
        pltpu.make_async_remote_copy(
            src_ref=terms_ref.at[other],
            dst_ref=landed.at[other],
            send_sem=term_send.at[other],
            recv_sem=term_recv.at[other],
            device_id={"inst": other},
            device_id_type=MESH,
        ).wait()
        return 0

    lax.fori_loop(1, members, take_term, 0)
    shared[group] = jnp.sum(landed[...], axis=0)

    def share(k, other_slot):
        other = lax.rem(group + k, groups)
        return pltpu.make_async_remote_copy(
            src_ref=shared.at[group],
            dst_ref=shared.at[other if other_slot else group],
            send_sem=share_send.at[other],
            recv_sem=share_recv.at[other if other_slot else group],
            device_id={"tp": other},
            device_id_type=MESH,
        )

    def send_share(k, _):
        share(k, False).start()
        return 0

    lax.fori_loop(1, groups, send_share, 0)
    lax.fori_loop(LAG, rounds, steady, 0)
    lax.fori_loop(rounds, rounds + LAG, closing, 0)

    their_base, their_count = info_ref[2], info_ref[3]
    my_base, my_count = info_ref[0], info_ref[1]

    def gather_theirs(b, _):
        theirs[b] = store[jnp.where(b < their_count, their_base + b, zero)]
        return 0

    lax.fori_loop(0, depth, gather_theirs, 0)
    give = pltpu.make_async_remote_copy(
        src_ref=theirs,
        dst_ref=out_ref.at[:, core],
        send_sem=swap_sems.at[2],
        recv_sem=swap_sems.at[3],
        device_id={"inst": partner},
        device_id_type=MESH,
    )
    give.start()

    def gather_mine(b, _):
        mine[b] = store[jnp.where(b < my_count, my_base + b, zero)]
        return 0

    lax.fori_loop(0, depth, gather_mine, 0)
    write = pltpu.make_async_copy(mine, out_ref.at[:, core], swap_sems.at[4])
    write.start()

    def take_share(k, _):
        share(k, True).wait()
        return 0

    lax.fori_loop(1, groups, take_share, 0)
    sums_ref[...] = jnp.sum(shared[...], axis=0)
    give.wait_send()
    pltpu.make_async_remote_copy(
        src_ref=theirs,
        dst_ref=out_ref.at[:, 1 - core],
        send_sem=swap_sems.at[2],
        recv_sem=swap_sems.at[3],
        device_id={"inst": partner},
        device_id_type=MESH,
    ).wait_recv()
    write.wait()


def route(index, rounds, members, groups, table, info, staged, terms):
    layers, depth, tall, width = staged.shape
    smem = pl.BlockSpec(memory_space=pltpu.SMEM)
    vmem = pl.BlockSpec(memory_space=pltpu.VMEM)
    unit = (tall, width)
    dma = pltpu.SemaphoreType.DMA
    return pl.pallas_call(
        functools.partial(route_kernel, rounds, members, groups),
        out_shape=(
            jax.ShapeDtypeStruct((depth, layers) + unit, staged.dtype),
            jax.ShapeDtypeStruct(terms.shape[1:], terms.dtype),
        ),
        in_specs=[smem, smem, vmem, vmem],
        out_specs=(pl.BlockSpec(memory_space=pl.ANY), vmem),
        scratch_shapes=[
            pltpu.VMEM((2 * depth + 3 * RMAX + 1,) + unit, staged.dtype),
            pltpu.VMEM((3, LAG) + unit, staged.dtype),
            pltpu.VMEM((3, 2 * LAG) + unit, staged.dtype),
            pltpu.VMEM((depth,) + unit, staged.dtype),
            pltpu.VMEM((depth,) + unit, staged.dtype),
            pltpu.VMEM(terms.shape, terms.dtype),
            pltpu.VMEM((groups,) + terms.shape[1:], terms.dtype),
            dma((5,)),
            dma((3, LAG)),
            dma((3, 2 * LAG)),
            dma((members,)),
            dma((members,)),
            dma((groups,)),
            dma((groups,)),
        ],
        compiler_params=pltpu.CompilerParams(
            collective_id=index, has_side_effects=True, vmem_limit_bytes=VMEM_LIMIT
        ),
        name="route_%d" % rounds,
    )(table, info, staged, terms)


def relay(staged, source, target, members):
    place = lax.axis_index("inst")
    request_ids = jnp.arange(source.shape[0], dtype=jnp.int32)
    incoming = jnp.sum(jnp.where(target == place, request_ids, 0))
    blocks = jnp.swapaxes(staged, 0, 1)
    depth = blocks.shape[0]
    sender = source[incoming]
    share = depth // members
    relays = jnp.arange(members, dtype=jnp.int32)
    grouped = blocks.reshape((members, share) + blocks.shape[1:])
    outgoing = grouped[(relays - place) % members]
    source_of = jnp.sum(
        jnp.where(target[None, :] == relays[:, None], source[None, :], 0), axis=1
    )
    gather_back = (sender + relays) % members
    sectioned = lax.all_to_all(outgoing, "inst", split_axis=0, concat_axis=0, tiled=True)
    landed = lax.all_to_all(sectioned[source_of], "inst", split_axis=0, concat_axis=0, tiled=True)
    return landed[gather_back].reshape(blocks.shape)


def decode_attention(queries, cache_keys, cache_values, new_keys, new_values):
    layers, steps, requests, qwidth = queries.shape
    context = cache_keys.shape[2]
    kwidth = cache_keys.shape[3]
    heads_local = kwidth // HD
    grouping = qwidth // kwidth
    query = queries.reshape(layers, steps, requests, heads_local, grouping, HD)
    keyed = cache_keys.reshape(layers, requests, context, heads_local, HD)
    valued = cache_values.reshape(layers, requests, context, heads_local, HD)
    fresh_keys = new_keys.reshape(layers, steps, requests, heads_local, HD)
    fresh_values = new_values.reshape(layers, steps, requests, heads_local, HD)
    factor = 1.0 / math.sqrt(HD)
    old_scores = (
        jnp.einsum("lsrkgd,lrckd->lsrkgc", query, keyed, preferred_element_type=jnp.float32)
        * factor
    )
    new_scores = (
        jnp.einsum("lsrkgd,ltrkd->lsrkgt", query, fresh_keys, preferred_element_type=jnp.float32)
        * factor
    )
    order = jnp.arange(steps)
    visible = (order[None, :] <= order[:, None])[None, :, None, None, None, :]
    new_scores = jnp.where(visible, new_scores, -1e30)
    highest = jnp.maximum(
        jnp.max(old_scores, axis=-1, keepdims=True), jnp.max(new_scores, axis=-1, keepdims=True)
    )
    old_exp = jnp.exp(old_scores - highest)
    new_exp = jnp.where(visible, jnp.exp(new_scores - highest), 0.0)
    denominator = jnp.sum(old_exp, axis=-1, keepdims=True) + jnp.sum(
        new_exp, axis=-1, keepdims=True
    )
    old_weights = (old_exp / denominator).astype(jnp.bfloat16)
    new_weights = (new_exp / denominator).astype(jnp.bfloat16)
    mixed = jnp.einsum(
        "lsrkgc,lrckd->lsrkgd", old_weights, valued, preferred_element_type=jnp.float32
    )
    mixed = mixed + jnp.einsum(
        "lsrkgt,ltrkd->lsrkgd", new_weights, fresh_values, preferred_element_type=jnp.float32
    )
    return mixed.astype(jnp.bfloat16).reshape(layers, steps, requests, qwidth)


def local(
    queries,
    cache_keys,
    cache_values,
    new_keys,
    new_values,
    kv_pool,
    mig_lengths,
    mig_source,
    mig_target,
    block_lists,
    owner_map,
    check_key,
):
    members = lax.axis_size("inst")
    groups = lax.axis_size("tp")
    place = lax.axis_index("inst")
    pool_blocks, layers, kinds, span, width = kv_pool.shape
    pool = kv_pool.reshape(pool_blocks, layers, kinds * span, width)
    table, info, staged, digest = plan(
        mig_lengths, mig_source, mig_target, block_lists, pool, check_key, members
    )
    request_ids = jnp.arange(mig_source.shape[0], dtype=jnp.int32)
    own_request = jnp.sum(jnp.where(mig_source == place, request_ids, 0))
    owners = owner_map[own_request]
    padded = 8 * members
    rows = (owners // SLOTS) * 8 + owners % SLOTS
    one_hot = (rows[None, :] == jnp.arange(padded)[:, None]).astype(jnp.float32)
    terms = jnp.dot(
        one_hot, digest, precision=lax.Precision.HIGHEST, preferred_element_type=jnp.float32
    ).reshape(members, 8, digest.shape[-1])

    def direct(index, rounds):
        def branch(operands):
            table, info, staged, terms = operands
            return route(index, rounds, members, groups, table, info, staged, terms)

        return branch

    def indirect(operands):
        table, info, staged, terms = operands
        summed = lax.psum(terms, "tp")
        mine = lax.psum_scatter(summed, "inst", scatter_dimension=0, tiled=True)
        return relay(staged, mig_source, mig_target, members), mine.reshape(terms.shape[1:])

    branches = [direct(index, rounds) for index, rounds in enumerate(ROUNDS)] + [indirect]
    arrived, sums = lax.switch(info[4], branches, (table, info, staged, terms))
    attention = decode_attention(queries, cache_keys, cache_values, new_keys, new_values)
    arrived = arrived.reshape((arrived.shape[0],) + kv_pool.shape[1:])
    return (attention, arrived, sums[:SLOTS])


def solution(mesh):
    placed = (
        P(None, None, "inst", "tp"),
        P(None, "inst", None, "tp"),
        P(None, "inst", None, "tp"),
        P(None, None, "inst", "tp"),
        P(None, None, "inst", "tp"),
        P("inst", None, None, None, "tp"),
        P(),
        P(),
        P(),
        P(),
        P(),
        P(None, None, "tp", None),
    )
    return jax.shard_map(
        local,
        mesh=mesh,
        in_specs=placed,
        out_specs=(P(None, None, "inst", "tp"), P("inst", None, None, None, "tp"), P("inst", None)),
        check_vma=False,
    )
```

```python
import functools
import math

import jax
import jax.numpy as jnp
from jax import lax
from jax.experimental import pallas as pl
from jax.experimental.pallas import tpu as pltpu
from jax.sharding import PartitionSpec as P

HD = 128
SLOTS = 2
STEPS = 4
LAG = 6
ROUNDS = (104, 122, 140, 164, 232)
PIECES = 4
RMAX = ROUNDS[-1]
VMEM_LIMIT = 60 * 1024 * 1024
MESH = pl.DeviceIdType.MESH


def plan_kernel(
    members,
    len_ref,
    src_ref,
    tgt_ref,
    list_ref,
    pool_ref,
    table_ref,
    info_ref,
    staged_ref,
    free,
    done,
    sem,
):
    me = lax.axis_index("inst")
    requests = len_ref.shape[0]
    depth = list_ref.shape[1]
    span = staged_ref.shape[2] // 2
    chip = me // 2
    rows = members // 4

    def find(r, found):
        return jnp.where(src_ref[r] == me, r, found)

    own = lax.fori_loop(0, requests, find, jnp.int32(0))

    def fetch(b, _):
        pltpu.make_async_copy(pool_ref.at[list_ref[own, b]], staged_ref.at[:, b], sem).start()
        return 0

    lax.fori_loop(0, depth, fetch, 0)

    def clear(i, _):
        table_ref[i] = 0
        return 0

    lax.fori_loop(0, table_ref.shape[0], clear, 0)

    def clear_free(i, _):
        free[i] = 0
        return 0

    lax.fori_loop(0, free.shape[0], clear_free, 0)

    def clear_done(i, _):
        done[i] = 0
        return 0

    lax.fori_loop(0, requests, clear_done, 0)
    for i in range(8):
        info_ref[i] = 0

    def schedule(_, longest):
        def pick(r, best):
            score = jnp.where(done[r] == 0, len_ref[r], 0)
            better = score > best[0]
            return jnp.where(better, score, best[0]), jnp.where(better, r, best[1])

        tokens, r = lax.fori_loop(0, requests, pick, (jnp.int32(0), jnp.int32(0)))
        done[r] = 1
        count = (tokens + span - 1) // span
        source, target = src_ref[r], tgt_ref[r]
        from_row, from_col = source // 4, (source // 2) % 2
        to_row, to_col = target // 4, (target // 2) % 2
        cross = from_col != to_col
        up = to_row > from_row
        hops = jnp.abs(to_row - from_row)
        step = jnp.where(up, 1, -1)
        port = jnp.where(up, 0, 1)

        def slot(link, ready):
            return jnp.maximum(ready, free[link])

        def zlink(col, row):
            return (port * 2 + col) * rows + row

        def xlink(col, row):
            return (4 + col) * rows + row

        def run(col, ready, last):
            def hop(i, state):
                ready, _ = state
                begin = slot(zlink(col, from_row + i * step), ready)
                return begin + LAG, begin

            return lax.fori_loop(0, hops, hop, (ready, last))

        def finish(col):
            out = from_col != col
            back = to_col != col
            begin = slot(xlink(from_col, from_row), jnp.int32(0))
            last = jnp.where(out, begin, 0)
            ready, last = run(col, jnp.where(out, begin + LAG, 0), last)
            begin = slot(xlink(col, to_row), ready)
            return jnp.where(back, begin, last)

        moves = jnp.logical_or(hops > 0, cross)
        swerve = jnp.logical_and(moves, finish(1 - from_col) < finish(from_col))
        lane = jnp.where(swerve, 1 - from_col, from_col)

        first_base = jnp.where(source == me, 0, depth)

        def take(link, sender, way, ready, base):
            begin = slot(link, ready)
            free[link] = begin + count

            @pl.when(jnp.logical_and(sender == chip, begin + count <= RMAX))
            def _():
                def fill(i, _):
                    table_ref[way * RMAX + begin + i] = base + i
                    return 0

                lax.fori_loop(0, count, fill, 0)

            return (
                begin + LAG,
                2 * depth + way * RMAX + begin,
                jnp.maximum(begin + count, 0),
            )

        def x_move(needed, col, row, state):
            return lax.cond(
                needed,
                lambda s: take(xlink(col, row), row * 2 + col, 2, s[0], s[1]),
                lambda s: s,
                state,
            )

        def z_hop(i, s):
            row = from_row + i * step
            return take(zlink(lane, row), row * 2 + lane, port, s[0], s[1])

        state = (jnp.int32(0), first_base, jnp.int32(0))
        state = x_move(from_col != lane, from_col, from_row, state)
        state = lax.fori_loop(0, hops, z_hop, state)
        state = x_move(to_col != lane, lane, to_row, state)
        _, base, end = state

        @pl.when(target == me)
        def _():
            info_ref[0] = base
            info_ref[1] = count

        @pl.when(jnp.logical_and(target // 2 == chip, target != me))
        def _():
            info_ref[2] = base
            info_ref[3] = count

        return jnp.maximum(longest, end)

    longest = lax.fori_loop(0, requests, schedule, jnp.int32(0))
    choice = jnp.int32(0)
    for size in ROUNDS:
        choice = choice + jnp.where(longest > size, 1, 0)
    info_ref[4] = choice
    info_ref[5] = longest

    pltpu.make_async_copy(staged_ref, staged_ref, sem).wait()
    length = len_ref[own]

    def mask(b, _):
        block = staged_ref[:, b]
        token = lax.rem(lax.broadcasted_iota(jnp.int32, block.shape, 1), span) + b * span
        staged_ref[:, b] = jnp.where(token < length, block, jnp.zeros_like(block))
        return 0

    lax.fori_loop(length // span, depth, mask, 0)


def plan(lengths, source, target, lists, pool, members):
    depth = lists.shape[1]
    layers, width = pool.shape[1], pool.shape[3]
    smem = pl.BlockSpec(memory_space=pltpu.SMEM)
    vmem = pl.BlockSpec(memory_space=pltpu.VMEM)
    return pl.pallas_call(
        functools.partial(plan_kernel, members),
        out_shape=(
            jax.ShapeDtypeStruct((3 * RMAX,), jnp.int32),
            jax.ShapeDtypeStruct((8,), jnp.int32),
            jax.ShapeDtypeStruct((layers, depth, pool.shape[2], width), pool.dtype),
        ),
        in_specs=[smem, smem, smem, smem, pl.BlockSpec(memory_space=pl.ANY)],
        out_specs=(smem, smem, vmem),
        scratch_shapes=[
            pltpu.SMEM((6 * (members // 4),), jnp.int32),
            pltpu.SMEM((lengths.shape[0],), jnp.int32),
            pltpu.SemaphoreType.DMA,
        ],
        compiler_params=pltpu.CompilerParams(vmem_limit_bytes=VMEM_LIMIT),
        name="plan",
    )(lengths, source, target, lists, pool)


def route_kernel(
    rounds,
    members,
    groups,
    table_ref,
    info_ref,
    staged_ref,
    source_ref,
    owner_ref,
    key_ref,
    query_ref,
    new_keys_ref,
    new_values_ref,
    cache_keys_ref,
    cache_values_ref,
    out_ref,
    sums_ref,
    mixed_ref,
    store,
    stage,
    ring,
    theirs,
    mine,
    cache_keys,
    cache_values,
    digests,
    terms_ref,
    landed,
    shared,
    swap_sems,
    cache_sems,
    stage_sems,
    ring_sems,
    term_send,
    term_recv,
    share_send,
    share_recv,
):
    me = lax.axis_index("inst")
    group = lax.axis_index("tp")
    core, row = me % 2, me // 4
    depth = staged_ref.shape[1]
    zero = store.shape[0] - 1
    partner = me + 1 - 2 * core
    beside = me + 2 - 4 * ((me // 2) % 2)
    has_up = row < members // 4 - 1
    has_down = row > 0
    ways = (
        (0, me + 4, has_up, has_down),
        (1, me - 4, has_down, has_up),
        (2, beside, None, None),
    )

    def when(condition, body):
        if condition is None:
            body()
        else:
            pl.when(condition)(body)

    load_keys = pltpu.make_async_copy(cache_keys_ref, cache_keys, cache_sems.at[0])
    load_values = pltpu.make_async_copy(cache_values_ref, cache_values, cache_sems.at[1])
    load_keys.start()
    load_values.start()
    barrier = pltpu.get_barrier_semaphore()

    def greet(k, _):
        pl.semaphore_signal(
            barrier, inc=1, device_id={"inst": lax.rem(me + k, members)}, device_id_type=MESH
        )
        return 0

    def greet_group(k, _):
        pl.semaphore_signal(
            barrier, inc=1, device_id={"tp": lax.rem(group + k, groups)}, device_id_type=MESH
        )
        return 0

    lax.fori_loop(1, members, greet, 0)
    lax.fori_loop(1, groups, greet_group, 0)
    pl.semaphore_wait(barrier, members + groups - 2)

    swap = pltpu.make_async_remote_copy(
        src_ref=staged_ref.at[1 - core],
        dst_ref=store.at[pl.ds(depth, depth)],
        send_sem=swap_sems.at[0],
        recv_sem=swap_sems.at[1],
        device_id={"inst": partner},
        device_id_type=MESH,
    )
    swap.start()

    def term(k):
        other = lax.rem(me + k, members)
        return pltpu.make_async_remote_copy(
            src_ref=terms_ref.at[other],
            dst_ref=landed.at[me],
            send_sem=term_send.at[other],
            recv_sem=term_recv.at[me],
            device_id={"inst": other},
            device_id_type=MESH,
        )

    def send_term(k, _):
        term(k).start()
        return 0

    def keep(b, _):
        store[b] = staged_ref[core, b]
        return 0

    lax.fori_loop(0, depth, keep, 0)
    store[zero] = jnp.zeros(store.shape[1:], store.dtype)
    swap.wait()

    def hand(way, to, t):
        return pltpu.make_async_remote_copy(
            src_ref=stage.at[way, lax.rem(t, LAG)],
            dst_ref=ring.at[way, lax.rem(t, 2 * LAG)],
            send_sem=stage_sems.at[way, lax.rem(t, LAG)],
            recv_sem=ring_sems.at[way, lax.rem(t, 2 * LAG)],
            device_id={"inst": to},
            device_id_type=MESH,
        )

    def receive(t):
        for way, to, sends, receives in ways:

            def body(way=way, to=to):
                hand(way, to, t).wait_recv()
                store[2 * depth + way * RMAX + t] = ring[way, lax.rem(t, 2 * LAG)]

            when(receives, body)

    def release(t):
        for way, to, sends, receives in ways:

            def body(way=way, to=to):
                hand(way, to, t).wait_send()

            when(sends, body)

    def send(t):
        for way, to, sends, receives in ways:

            def body(way=way, to=to):
                stage[way, lax.rem(t, LAG)] = store[table_ref[way * RMAX + t]]
                hand(way, to, t).start()

            when(sends, body)

    def opening(t, _):
        send(t)
        return 0

    def steady(t, _):
        receive(t - LAG)
        release(t - LAG)
        send(t)
        return 0

    def closing(t, _):
        receive(t - LAG)
        release(t - LAG)
        return 0

    lax.fori_loop(0, LAG, opening, 0)

    group_size = 8
    span = staged_ref.shape[2] // 2
    heads = staged_ref.shape[3] // HD

    def digest(i):
        total = jnp.zeros((group_size * span, key_ref.shape[-1]), jnp.float32)
        at = pl.ds(pl.multiple_of(i * group_size, group_size), group_size)
        for layer in range(staged_ref.shape[0]):
            for kind in range(2):
                for head in range(heads):
                    lanes = pl.ds(head * HD, HD)
                    part = staged_ref[layer, at, pl.ds(kind * span, span), lanes]
                    projected = jnp.dot(
                        part.reshape(group_size * span, HD),
                        key_ref[layer, kind, lanes, :],
                        preferred_element_type=jnp.float32,
                    )
                    total = total + jnp.tanh(projected)
        digests[at, :] = jnp.sum(total.reshape(group_size, span, -1), axis=1) * (1.0 / 16.0)

    def digest_turn(i, _):
        for j in range(2):
            steady(LAG + 2 * i + j, 0)
        digest(i)
        return 0

    digest_turns = depth // group_size
    lax.fori_loop(0, digest_turns, digest_turn, 0)

    owners = jnp.sum(
        jnp.where(source_ref[...] == me, owner_ref[...], 0), axis=0, keepdims=True
    )
    spot = lax.bitwise_and(owners, SLOTS - 1)
    spot = (owners - spot) * (8 // SLOTS) + spot
    tall = 8 * members
    one_hot = jnp.where(
        lax.broadcasted_iota(jnp.int32, (tall, depth), 0) == spot, 1.0, 0.0
    ).astype(jnp.float32)
    terms_ref[...] = jnp.dot(
        one_hot,
        digests[...],
        precision=lax.Precision.HIGHEST,
        preferred_element_type=jnp.float32,
    ).reshape(terms_ref.shape)
    landed[me] = terms_ref[me]
    lax.fori_loop(1, members, send_term, 0)
    load_keys.wait()
    load_values.wait()

    items, _, lines, _ = query_ref.shape
    fresh = new_keys_ref.shape[1]
    grouping = lines // STEPS
    last_dims = (((1,), (1,)), ((), ()))

    def attend(i):
        step = lax.broadcasted_iota(jnp.int32, (lines, fresh), 0) // grouping
        visible = lax.broadcasted_iota(jnp.int32, (lines, fresh), 1) <= step
        for head in range(heads):
            lanes = pl.ds(head * HD, HD)
            query = query_ref[i, head]
            old = lax.dot_general(
                query, cache_keys[i, :, lanes], last_dims, preferred_element_type=jnp.float32
            ) * (1.0 / math.sqrt(HD))
            new = lax.dot_general(
                query, new_keys_ref[i, :, lanes], last_dims, preferred_element_type=jnp.float32
            ) * (1.0 / math.sqrt(HD))
            new = jnp.where(visible, new, -1e30)
            highest = jnp.maximum(
                jnp.max(old, axis=1, keepdims=True), jnp.max(new, axis=1, keepdims=True)
            )
            old = jnp.exp(old - highest)
            new = jnp.where(visible, jnp.exp(new - highest), 0.0)
            denominator = jnp.sum(old, axis=1, keepdims=True) + jnp.sum(
                new, axis=1, keepdims=True
            )
            mixed = jnp.dot(
                (old / denominator).astype(jnp.bfloat16),
                cache_values[i, :, lanes],
                preferred_element_type=jnp.float32,
            ) + jnp.dot(
                (new / denominator).astype(jnp.bfloat16),
                new_values_ref[i, :, lanes],
                preferred_element_type=jnp.float32,
            )
            mixed_ref[i, head] = mixed.astype(jnp.bfloat16)

    attend_from = LAG + 2 * digest_turns

    def attend_turn(i, _):
        for j in range(3):
            steady(attend_from + 3 * i + j, 0)
        attend(i)
        return 0

    lax.fori_loop(0, items, attend_turn, 0)
    plain_from = attend_from + 3 * items

    def take_term(k, _):
        other = lax.rem(me + k, members)
        pltpu.make_async_remote_copy(
            src_ref=terms_ref.at[other],
            dst_ref=landed.at[other],
            send_sem=term_send.at[other],
            recv_sem=term_recv.at[other],
            device_id={"inst": other},
            device_id_type=MESH,
        ).wait()
        return 0

    lax.fori_loop(1, members, take_term, 0)
    shared[group] = jnp.sum(landed[...], axis=0)

    def share(k, other_slot):
        other = lax.rem(group + k, groups)
        return pltpu.make_async_remote_copy(
            src_ref=shared.at[group],
            dst_ref=shared.at[other if other_slot else group],
            send_sem=share_send.at[other],
            recv_sem=share_recv.at[other if other_slot else group],
            device_id={"tp": other},
            device_id_type=MESH,
        )

    def send_share(k, _):
        share(k, False).start()
        return 0

    lax.fori_loop(1, groups, send_share, 0)
    lax.fori_loop(plain_from, rounds, steady, 0)
    lax.fori_loop(rounds, rounds + LAG, closing, 0)

    their_base, their_count = info_ref[2], info_ref[3]
    my_base, my_count = info_ref[0], info_ref[1]

    piece = depth // PIECES

    def gather(box, base, count):
        def body(b, _):
            box[b] = store[jnp.where(b < count, base + b, zero)]
            return 0

        return body

    def give(k, layer):
        part = pl.ds(k * piece, piece)
        return pltpu.make_async_remote_copy(
            src_ref=theirs.at[part],
            dst_ref=out_ref.at[part, layer],
            send_sem=swap_sems.at[2 + k],
            recv_sem=swap_sems.at[2 + PIECES + k],
            device_id={"inst": partner},
            device_id_type=MESH,
        )

    def write(k):
        part = pl.ds(k * piece, piece)
        return pltpu.make_async_copy(
            mine.at[part], out_ref.at[part, core], swap_sems.at[2 + 2 * PIECES + k]
        )

    for k in range(PIECES):
        lax.fori_loop(
            k * piece, (k + 1) * piece, gather(theirs, their_base, their_count), 0
        )
        give(k, core).start()
    for k in range(PIECES):
        lax.fori_loop(k * piece, (k + 1) * piece, gather(mine, my_base, my_count), 0)
        write(k).start()

    def take_share(k, _):
        share(k, True).wait()
        return 0

    lax.fori_loop(1, groups, take_share, 0)
    sums_ref[...] = jnp.sum(shared[...], axis=0)
    for k in range(PIECES):
        give(k, core).wait_send()
        give(k, 1 - core).wait_recv()
        write(k).wait()


def route(index, rounds, members, groups, operands):
    staged, key, query, cache = operands[2], operands[5], operands[6], operands[9]
    layers, depth, tall, width = staged.shape
    smem = pl.BlockSpec(memory_space=pltpu.SMEM)
    vmem = pl.BlockSpec(memory_space=pltpu.VMEM)
    hbm = pl.BlockSpec(memory_space=pl.ANY)
    unit = (tall, width)
    entry = (8, key.shape[-1])
    dma = pltpu.SemaphoreType.DMA
    return pl.pallas_call(
        functools.partial(route_kernel, rounds, members, groups),
        out_shape=(
            jax.ShapeDtypeStruct((depth, layers) + unit, staged.dtype),
            jax.ShapeDtypeStruct(entry, jnp.float32),
            jax.ShapeDtypeStruct(query.shape, query.dtype),
        ),
        in_specs=[smem, smem] + [vmem] * 7 + [hbm, hbm],
        out_specs=(hbm, vmem, vmem),
        scratch_shapes=[
            pltpu.VMEM((2 * depth + 3 * RMAX + 1,) + unit, staged.dtype),
            pltpu.VMEM((3, LAG) + unit, staged.dtype),
            pltpu.VMEM((3, 2 * LAG) + unit, staged.dtype),
            pltpu.VMEM((depth,) + unit, staged.dtype),
            pltpu.VMEM((depth,) + unit, staged.dtype),
            pltpu.VMEM(cache.shape, cache.dtype),
            pltpu.VMEM(cache.shape, cache.dtype),
            pltpu.VMEM((depth, key.shape[-1]), jnp.float32),
            pltpu.VMEM((members,) + entry, jnp.float32),
            pltpu.VMEM((members,) + entry, jnp.float32),
            pltpu.VMEM((groups,) + entry, jnp.float32),
            dma((2 + 3 * PIECES,)),
            dma((2,)),
            dma((3, LAG)),
            dma((3, 2 * LAG)),
            dma((members,)),
            dma((members,)),
            dma((groups,)),
            dma((groups,)),
        ],
        compiler_params=pltpu.CompilerParams(
            collective_id=index, has_side_effects=True, vmem_limit_bytes=VMEM_LIMIT
        ),
        name="route_%d" % rounds,
    )(*operands)


def relay(staged, source, target, members):
    place = lax.axis_index("inst")
    request_ids = jnp.arange(source.shape[0], dtype=jnp.int32)
    incoming = jnp.sum(jnp.where(target == place, request_ids, 0))
    blocks = jnp.swapaxes(staged, 0, 1)
    depth = blocks.shape[0]
    sender = source[incoming]
    share = depth // members
    relays = jnp.arange(members, dtype=jnp.int32)
    grouped = blocks.reshape((members, share) + blocks.shape[1:])
    outgoing = grouped[(relays - place) % members]
    source_of = jnp.sum(
        jnp.where(target[None, :] == relays[:, None], source[None, :], 0), axis=1
    )
    gather_back = (sender + relays) % members
    sectioned = lax.all_to_all(outgoing, "inst", split_axis=0, concat_axis=0, tiled=True)
    landed = lax.all_to_all(sectioned[source_of], "inst", split_axis=0, concat_axis=0, tiled=True)
    return landed[gather_back].reshape(blocks.shape)


def decode_attention(queries, cache_keys, cache_values, new_keys, new_values):
    layers, steps, requests, qwidth = queries.shape
    context = cache_keys.shape[2]
    kwidth = cache_keys.shape[3]
    heads_local = kwidth // HD
    grouping = qwidth // kwidth
    query = queries.reshape(layers, steps, requests, heads_local, grouping, HD)
    keyed = cache_keys.reshape(layers, requests, context, heads_local, HD)
    valued = cache_values.reshape(layers, requests, context, heads_local, HD)
    fresh_keys = new_keys.reshape(layers, steps, requests, heads_local, HD)
    fresh_values = new_values.reshape(layers, steps, requests, heads_local, HD)
    factor = 1.0 / math.sqrt(HD)
    old_scores = (
        jnp.einsum("lsrkgd,lrckd->lsrkgc", query, keyed, preferred_element_type=jnp.float32)
        * factor
    )
    new_scores = (
        jnp.einsum("lsrkgd,ltrkd->lsrkgt", query, fresh_keys, preferred_element_type=jnp.float32)
        * factor
    )
    order = jnp.arange(steps)
    visible = (order[None, :] <= order[:, None])[None, :, None, None, None, :]
    new_scores = jnp.where(visible, new_scores, -1e30)
    highest = jnp.maximum(
        jnp.max(old_scores, axis=-1, keepdims=True), jnp.max(new_scores, axis=-1, keepdims=True)
    )
    old_exp = jnp.exp(old_scores - highest)
    new_exp = jnp.where(visible, jnp.exp(new_scores - highest), 0.0)
    denominator = jnp.sum(old_exp, axis=-1, keepdims=True) + jnp.sum(
        new_exp, axis=-1, keepdims=True
    )
    old_weights = (old_exp / denominator).astype(jnp.bfloat16)
    new_weights = (new_exp / denominator).astype(jnp.bfloat16)
    mixed = jnp.einsum(
        "lsrkgc,lrckd->lsrkgd", old_weights, valued, preferred_element_type=jnp.float32
    )
    mixed = mixed + jnp.einsum(
        "lsrkgt,ltrkd->lsrkgd", new_weights, fresh_values, preferred_element_type=jnp.float32
    )
    return mixed.astype(jnp.bfloat16).reshape(layers, steps, requests, qwidth)


def local(
    queries,
    cache_keys,
    cache_values,
    new_keys,
    new_values,
    kv_pool,
    mig_lengths,
    mig_source,
    mig_target,
    block_lists,
    owner_map,
    check_key,
):
    members = lax.axis_size("inst")
    groups = lax.axis_size("tp")
    place = lax.axis_index("inst")
    pool_blocks, layers, kinds, span, width = kv_pool.shape
    pool = kv_pool.reshape(pool_blocks, layers, kinds * span, width)
    table, info, staged = plan(
        mig_lengths, mig_source, mig_target, block_lists, pool, members
    )
    layers, steps, requests, qwidth = queries.shape
    context = cache_keys.shape[2]
    heads = width // HD
    grouping = qwidth // width
    items = layers * requests
    lines = steps * grouping
    query = queries.reshape(layers, steps, requests, heads, grouping, HD)
    query = jnp.transpose(query, (0, 2, 3, 1, 4, 5)).reshape(items, heads, lines, HD)

    def pad(new):
        new = jnp.swapaxes(new, 1, 2).reshape(items, steps, width)
        return jnp.pad(new, ((0, 0), (0, 16 - steps), (0, 0)))

    operands = (
        table,
        info,
        staged,
        mig_source.reshape(-1, 1),
        owner_map,
        check_key,
        query,
        pad(new_keys),
        pad(new_values),
        cache_keys.reshape(items, context, width),
        cache_values.reshape(items, context, width),
    )

    def direct(index, rounds):
        return lambda operands: route(index, rounds, members, groups, operands)

    def indirect(operands):
        staged = operands[2]
        depth = staged.shape[1]
        grid = staged.reshape(layers, depth, kinds, span, heads, HD)
        projection = check_key.reshape(layers, kinds, heads, HD, -1)
        projected = jnp.einsum(
            "lbktgd,lkgde->blktge", grid, projection, preferred_element_type=jnp.float32
        )
        digest = jnp.sum(jnp.tanh(projected), axis=(1, 2, 3, 4)) / 16.0
        request_ids = jnp.arange(mig_source.shape[0], dtype=jnp.int32)
        own_request = jnp.sum(jnp.where(mig_source == place, request_ids, 0))
        owners = owner_map[own_request]
        rows = (owners // SLOTS) * 8 + owners % SLOTS
        one_hot = (rows[None, :] == jnp.arange(8 * members)[:, None]).astype(jnp.float32)
        terms = jnp.dot(
            one_hot, digest, precision=lax.Precision.HIGHEST, preferred_element_type=jnp.float32
        ).reshape(members, 8, digest.shape[-1])
        summed = lax.psum(terms, "tp")
        sums = lax.psum_scatter(summed, "inst", scatter_dimension=0, tiled=True)
        attention = decode_attention(queries, cache_keys, cache_values, new_keys, new_values)
        attention = attention.reshape(layers, steps, requests, heads, grouping, HD)
        attention = jnp.transpose(attention, (0, 2, 3, 1, 4, 5)).reshape(query.shape)
        moved = relay(staged, mig_source, mig_target, members)
        return moved, sums.reshape(terms.shape[1:]), attention

    branches = [direct(index, rounds) for index, rounds in enumerate(ROUNDS)] + [indirect]
    arrived, sums, mixed = lax.switch(info[4], branches, operands)
    arrived = arrived.reshape((arrived.shape[0],) + kv_pool.shape[1:])
    mixed = mixed.reshape(layers, requests, heads, steps, grouping, HD)
    attention = jnp.transpose(mixed, (0, 3, 1, 2, 4, 5)).reshape(queries.shape)
    return (attention, arrived, sums[:SLOTS])


def solution(mesh):
    placed = (
        P(None, None, "inst", "tp"),
        P(None, "inst", None, "tp"),
        P(None, "inst", None, "tp"),
        P(None, None, "inst", "tp"),
        P(None, None, "inst", "tp"),
        P("inst", None, None, None, "tp"),
        P(),
        P(),
        P(),
        P(),
        P(),
        P(None, None, "tp", None),
    )
    return jax.shard_map(
        local,
        mesh=mesh,
        in_specs=placed,
        out_specs=(P(None, None, "inst", "tp"), P("inst", None, None, None, "tp"), P("inst", None)),
        check_vma=False,
    )
```

```python
import functools
import math

import jax
import jax.numpy as jnp
from jax import lax
from jax.experimental import pallas as pl
from jax.experimental.pallas import tpu as pltpu
from jax.sharding import PartitionSpec as P

HD = 128
SLOTS = 2
STEPS = 4
LAG = 5
ROUNDS = (98, 110, 122, 134, 148, 172, 232)
PIECES = 4
BATCH = 8
RMAX = ROUNDS[-1]
VMEM_LIMIT = 60 * 1024 * 1024
MESH = pl.DeviceIdType.MESH


def plan_kernel(
    members,
    len_ref,
    src_ref,
    tgt_ref,
    list_ref,
    pool_ref,
    table_ref,
    info_ref,
    staged_ref,
    free,
    done,
    sem,
):
    me = lax.axis_index("inst")
    requests = len_ref.shape[0]
    depth = list_ref.shape[1]
    span = staged_ref.shape[2] // 2
    chip = me // 2
    rows = members // 4

    def find(r, found):
        return jnp.where(src_ref[r] == me, r, found)

    own = lax.fori_loop(0, requests, find, jnp.int32(0))

    def fetch(b, _):
        pltpu.make_async_copy(pool_ref.at[list_ref[own, b]], staged_ref.at[:, b], sem).start()
        return 0

    lax.fori_loop(0, depth, fetch, 0)

    def clear(i, _):
        table_ref[i] = 0
        return 0

    lax.fori_loop(0, table_ref.shape[0], clear, 0, unroll=8)

    def clear_free(i, _):
        free[i] = 0
        return 0

    lax.fori_loop(0, free.shape[0], clear_free, 0)

    def clear_done(i, _):
        done[i] = 0
        return 0

    lax.fori_loop(0, requests, clear_done, 0)
    for i in range(8):
        info_ref[i] = 0

    def schedule(_, longest):
        def pick(r, best):
            score = jnp.where(done[r] == 0, len_ref[r], 0)
            better = score > best[0]
            return jnp.where(better, score, best[0]), jnp.where(better, r, best[1])

        tokens, r = lax.fori_loop(
            0, requests, pick, (jnp.int32(0), jnp.int32(0)), unroll=8
        )
        done[r] = 1
        count = (tokens + span - 1) // span
        source, target = src_ref[r], tgt_ref[r]
        from_row, from_col = source // 4, (source // 2) % 2
        to_row, to_col = target // 4, (target // 2) % 2
        cross = from_col != to_col
        up = to_row > from_row
        hops = jnp.abs(to_row - from_row)
        step = jnp.where(up, 1, -1)
        port = jnp.where(up, 0, 1)

        def slot(link, ready):
            return jnp.maximum(ready, free[link])

        def zlink(col, row):
            return (port * 2 + col) * rows + row

        def xlink(col, row):
            return (4 + col) * rows + row

        def run(col, ready, last):
            def hop(i, state):
                ready, _ = state
                begin = slot(zlink(col, from_row + i * step), ready)
                return begin + LAG, begin

            return lax.fori_loop(0, hops, hop, (ready, last))

        def finish(col):
            out = from_col != col
            back = to_col != col
            begin = slot(xlink(from_col, from_row), jnp.int32(0))
            last = jnp.where(out, begin, 0)
            ready, last = run(col, jnp.where(out, begin + LAG, 0), last)
            begin = slot(xlink(col, to_row), ready)
            return jnp.where(back, begin, last)

        moves = jnp.logical_or(hops > 0, cross)
        swerve = jnp.logical_and(moves, finish(1 - from_col) < finish(from_col))
        lane = jnp.where(swerve, 1 - from_col, from_col)

        first_base = jnp.where(source == me, 0, depth)

        def take(link, sender, way, ready, base):
            begin = slot(link, ready)
            free[link] = begin + count

            @pl.when(jnp.logical_and(sender == chip, begin + count <= RMAX))
            def _():
                def fill(i, _):
                    table_ref[way * RMAX + begin + i] = base + i
                    return 0

                lax.fori_loop(0, count, fill, 0)

            return (
                begin + LAG,
                2 * depth + way * RMAX + begin,
                jnp.maximum(begin + count, 0),
            )

        def x_move(needed, col, row, state):
            return lax.cond(
                needed,
                lambda s: take(xlink(col, row), row * 2 + col, 2, s[0], s[1]),
                lambda s: s,
                state,
            )

        def z_hop(i, s):
            row = from_row + i * step
            return take(zlink(lane, row), row * 2 + lane, port, s[0], s[1])

        state = (jnp.int32(0), first_base, jnp.int32(0))
        state = x_move(from_col != lane, from_col, from_row, state)
        state = lax.fori_loop(0, hops, z_hop, state)
        state = x_move(to_col != lane, lane, to_row, state)
        _, base, end = state

        @pl.when(target == me)
        def _():
            info_ref[0] = base
            info_ref[1] = count

        @pl.when(jnp.logical_and(target // 2 == chip, target != me))
        def _():
            info_ref[2] = base
            info_ref[3] = count

        return jnp.maximum(longest, end)

    longest = lax.fori_loop(0, requests, schedule, jnp.int32(0))
    choice = jnp.int32(0)
    for size in ROUNDS:
        choice = choice + jnp.where(longest > size, 1, 0)
    info_ref[4] = choice
    info_ref[5] = longest

    pltpu.make_async_copy(staged_ref, staged_ref, sem).wait()
    length = len_ref[own]

    def mask(b, _):
        block = staged_ref[:, b]
        token = lax.rem(lax.broadcasted_iota(jnp.int32, block.shape, 1), span) + b * span
        staged_ref[:, b] = jnp.where(token < length, block, jnp.zeros_like(block))
        return 0

    lax.fori_loop(length // span, depth, mask, 0)


def plan(lengths, source, target, lists, pool, members):
    depth = lists.shape[1]
    layers, width = pool.shape[1], pool.shape[3]
    smem = pl.BlockSpec(memory_space=pltpu.SMEM)
    vmem = pl.BlockSpec(memory_space=pltpu.VMEM)
    return pl.pallas_call(
        functools.partial(plan_kernel, members),
        out_shape=(
            jax.ShapeDtypeStruct((3 * RMAX,), jnp.int32),
            jax.ShapeDtypeStruct((8,), jnp.int32),
            jax.ShapeDtypeStruct((layers, depth, pool.shape[2], width), pool.dtype),
        ),
        in_specs=[smem, smem, smem, smem, pl.BlockSpec(memory_space=pl.ANY)],
        out_specs=(smem, smem, vmem),
        scratch_shapes=[
            pltpu.SMEM((6 * (members // 4),), jnp.int32),
            pltpu.SMEM((lengths.shape[0],), jnp.int32),
            pltpu.SemaphoreType.DMA,
        ],
        compiler_params=pltpu.CompilerParams(vmem_limit_bytes=VMEM_LIMIT),
        name="plan",
    )(lengths, source, target, lists, pool)


def route_kernel(
    rounds,
    members,
    groups,
    table_ref,
    info_ref,
    staged_ref,
    source_ref,
    owner_ref,
    key_ref,
    query_ref,
    new_keys_ref,
    new_values_ref,
    cache_keys_ref,
    cache_values_ref,
    out_ref,
    sums_ref,
    mixed_ref,
    store,
    stage,
    ring,
    theirs,
    mine,
    cache_keys,
    cache_values,
    digests,
    terms_ref,
    landed,
    shared,
    swap_sems,
    swap_sends,
    swap_recvs,
    cache_sems,
    stage_sems,
    ring_sems,
    term_send,
    term_recv,
    share_send,
    share_recv,
):
    me = lax.axis_index("inst")
    group = lax.axis_index("tp")
    core, row = me % 2, me // 4
    depth = staged_ref.shape[1]
    zero = store.shape[0] - 1
    partner = me + 1 - 2 * core
    beside = me + 2 - 4 * ((me // 2) % 2)
    has_up = row < members // 4 - 1
    has_down = row > 0
    ways = (
        (0, me + 4, has_up, has_down),
        (1, me - 4, has_down, has_up),
        (2, beside, None, None),
    )

    def when(condition, body):
        if condition is None:
            body()
        else:
            pl.when(condition)(body)

    load_keys = pltpu.make_async_copy(cache_keys_ref, cache_keys, cache_sems.at[0])
    load_values = pltpu.make_async_copy(cache_values_ref, cache_values, cache_sems.at[1])
    load_keys.start()
    load_values.start()
    barrier = pltpu.get_barrier_semaphore()

    def greet(k, _):
        pl.semaphore_signal(
            barrier, inc=1, device_id={"inst": lax.rem(me + k, members)}, device_id_type=MESH
        )
        return 0

    def greet_group(k, _):
        pl.semaphore_signal(
            barrier, inc=1, device_id={"tp": lax.rem(group + k, groups)}, device_id_type=MESH
        )
        return 0

    lax.fori_loop(1, members, greet, 0)
    lax.fori_loop(1, groups, greet_group, 0)
    pl.semaphore_wait(barrier, members + groups - 2)

    def swap(k):
        part = pl.ds(k * BATCH, BATCH)
        return pltpu.make_async_remote_copy(
            src_ref=staged_ref.at[1 - core, part],
            dst_ref=theirs.at[part],
            send_sem=swap_sends.at[k],
            recv_sem=swap_recvs.at[k],
            device_id={"inst": partner},
            device_id_type=MESH,
        )

    def accept(k):
        swap(k).wait()
        for j in range(BATCH):
            store[depth + k * BATCH + j] = theirs[k * BATCH + j]

    batches = depth // BATCH
    for k in range(batches):
        swap(k).start()

    def term(k):
        other = lax.rem(me + k, members)
        return pltpu.make_async_remote_copy(
            src_ref=terms_ref.at[other],
            dst_ref=landed.at[me],
            send_sem=term_send.at[other],
            recv_sem=term_recv.at[me],
            device_id={"inst": other},
            device_id_type=MESH,
        )

    def send_term(k, _):
        term(k).start()
        return 0

    def keep(b, _):
        store[b] = staged_ref[core, b]
        return 0

    lax.fori_loop(0, depth, keep, 0)
    store[zero] = jnp.zeros(store.shape[1:], store.dtype)
    accept(0)

    def hand(way, to, t):
        return pltpu.make_async_remote_copy(
            src_ref=stage.at[way, lax.rem(t, LAG)],
            dst_ref=ring.at[way, lax.rem(t, 2 * LAG)],
            send_sem=stage_sems.at[way, lax.rem(t, LAG)],
            recv_sem=ring_sems.at[way, lax.rem(t, 2 * LAG)],
            device_id={"inst": to},
            device_id_type=MESH,
        )

    def receive(t):
        for way, to, sends, receives in ways:

            def body(way=way, to=to):
                hand(way, to, t).wait_recv()
                store[2 * depth + way * RMAX + t] = ring[way, lax.rem(t, 2 * LAG)]

            when(receives, body)

    def release(t):
        for way, to, sends, receives in ways:

            def body(way=way, to=to):
                hand(way, to, t).wait_send()

            when(sends, body)

    def send(t):
        for way, to, sends, receives in ways:

            def body(way=way, to=to):
                stage[way, lax.rem(t, LAG)] = store[table_ref[way * RMAX + t]]
                hand(way, to, t).start()

            when(sends, body)

    def opening(t, _):
        send(t)
        return 0

    def steady(t, _):
        receive(t - LAG)
        release(t - LAG)
        send(t)
        return 0

    def closing(t, _):
        receive(t - LAG)
        release(t - LAG)
        return 0

    lax.fori_loop(0, LAG, opening, 0)

    group_size = BATCH
    span = staged_ref.shape[2] // 2
    heads = staged_ref.shape[3] // HD

    def digest(i):
        total = jnp.zeros((group_size * span, key_ref.shape[-1]), jnp.float32)
        at = pl.ds(pl.multiple_of(i * group_size, group_size), group_size)
        for layer in range(staged_ref.shape[0]):
            for kind in range(2):
                for head in range(heads):
                    lanes = pl.ds(head * HD, HD)
                    part = staged_ref[layer, at, pl.ds(kind * span, span), lanes]
                    projected = jnp.dot(
                        part.reshape(group_size * span, HD),
                        key_ref[layer, kind, lanes, :],
                        preferred_element_type=jnp.float32,
                    )
                    total = total + jnp.tanh(projected)
        digests[at, :] = jnp.sum(total.reshape(group_size, span, -1), axis=1) * (1.0 / 16.0)

    def digest_turn(i, _):
        pl.when(i + 1 < batches)(lambda: accept(i + 1))
        for j in range(2):
            steady(LAG + 2 * i + j, 0)
        digest(i)
        return 0

    lax.fori_loop(0, batches, digest_turn, 0)

    def own_row(r, row):
        return row + jnp.where(source_ref[r] == me, owner_ref[pl.ds(r, 1), :], 0)

    owners = lax.fori_loop(0, owner_ref.shape[0], own_row, jnp.zeros((1, depth), jnp.int32))
    spot = lax.bitwise_and(owners, SLOTS - 1)
    spot = (owners - spot) * (8 // SLOTS) + spot
    tall = 8 * members
    one_hot = jnp.where(
        lax.broadcasted_iota(jnp.int32, (tall, depth), 0) == spot, 1.0, 0.0
    ).astype(jnp.float32)
    terms_ref[...] = jnp.dot(
        one_hot,
        digests[...],
        precision=lax.Precision.HIGHEST,
        preferred_element_type=jnp.float32,
    ).reshape(terms_ref.shape)
    landed[me] = terms_ref[me]
    lax.fori_loop(1, members, send_term, 0)
    load_keys.wait()
    load_values.wait()

    items, _, lines, _ = query_ref.shape
    fresh = new_keys_ref.shape[1]
    grouping = lines // STEPS
    last_dims = (((1,), (1,)), ((), ()))

    def attend(i):
        step = lax.broadcasted_iota(jnp.int32, (lines, fresh), 0) // grouping
        visible = lax.broadcasted_iota(jnp.int32, (lines, fresh), 1) <= step
        for head in range(heads):
            lanes = pl.ds(head * HD, HD)
            query = query_ref[i, head]
            old = lax.dot_general(
                query, cache_keys[i, :, lanes], last_dims, preferred_element_type=jnp.float32
            ) * (1.0 / math.sqrt(HD))
            new = lax.dot_general(
                query, new_keys_ref[i, :, lanes], last_dims, preferred_element_type=jnp.float32
            ) * (1.0 / math.sqrt(HD))
            new = jnp.where(visible, new, -1e30)
            highest = jnp.maximum(
                jnp.max(old, axis=1, keepdims=True), jnp.max(new, axis=1, keepdims=True)
            )
            old = jnp.exp(old - highest)
            new = jnp.where(visible, jnp.exp(new - highest), 0.0)
            denominator = jnp.sum(old, axis=1, keepdims=True) + jnp.sum(
                new, axis=1, keepdims=True
            )
            mixed = jnp.dot(
                (old / denominator).astype(jnp.bfloat16),
                cache_values[i, :, lanes],
                preferred_element_type=jnp.float32,
            ) + jnp.dot(
                (new / denominator).astype(jnp.bfloat16),
                new_values_ref[i, :, lanes],
                preferred_element_type=jnp.float32,
            )
            mixed_ref[i, head] = mixed.astype(jnp.bfloat16)

    attend_from = LAG + 2 * batches

    def attend_turn(i, _):
        for j in range(3):
            steady(attend_from + 3 * i + j, 0)
        attend(i)
        return 0

    lax.fori_loop(0, items, attend_turn, 0)
    plain_from = attend_from + 3 * items

    def take_term(k, _):
        other = lax.rem(me + k, members)
        pltpu.make_async_remote_copy(
            src_ref=terms_ref.at[other],
            dst_ref=landed.at[other],
            send_sem=term_send.at[other],
            recv_sem=term_recv.at[other],
            device_id={"inst": other},
            device_id_type=MESH,
        ).wait()
        return 0

    lax.fori_loop(1, members, take_term, 0)
    shared[group] = jnp.sum(landed[...], axis=0)

    def share(k, other_slot):
        other = lax.rem(group + k, groups)
        return pltpu.make_async_remote_copy(
            src_ref=shared.at[group],
            dst_ref=shared.at[other if other_slot else group],
            send_sem=share_send.at[other],
            recv_sem=share_recv.at[other if other_slot else group],
            device_id={"tp": other},
            device_id_type=MESH,
        )

    def send_share(k, _):
        share(k, False).start()
        return 0

    lax.fori_loop(1, groups, send_share, 0)
    lax.fori_loop(plain_from, rounds, steady, 0)
    lax.fori_loop(rounds, rounds + LAG, closing, 0)

    their_base, their_count = info_ref[2], info_ref[3]
    my_base, my_count = info_ref[0], info_ref[1]

    piece = depth // PIECES

    def gather(box, base, count):
        def body(b, _):
            box[b] = store[jnp.where(b < count, base + b, zero)]
            return 0

        return body

    def give(k, layer):
        part = pl.ds(k * piece, piece)
        return pltpu.make_async_remote_copy(
            src_ref=theirs.at[part],
            dst_ref=out_ref.at[part, layer],
            send_sem=swap_sems.at[2 + k],
            recv_sem=swap_sems.at[2 + PIECES + k],
            device_id={"inst": partner},
            device_id_type=MESH,
        )

    def write(k):
        part = pl.ds(k * piece, piece)
        return pltpu.make_async_copy(
            mine.at[part], out_ref.at[part, core], swap_sems.at[2 + 2 * PIECES + k]
        )

    for k in range(PIECES):
        lax.fori_loop(
            k * piece, (k + 1) * piece, gather(theirs, their_base, their_count), 0
        )
        give(k, core).start()
    for k in range(PIECES):
        lax.fori_loop(k * piece, (k + 1) * piece, gather(mine, my_base, my_count), 0)
        write(k).start()

    def take_share(k, _):
        share(k, True).wait()
        return 0

    lax.fori_loop(1, groups, take_share, 0)
    sums_ref[...] = jnp.sum(shared[...], axis=0)
    for k in range(PIECES):
        give(k, core).wait_send()
        give(k, 1 - core).wait_recv()
        write(k).wait()


def route(index, rounds, members, groups, operands):
    staged, key, query, cache = operands[2], operands[5], operands[6], operands[9]
    layers, depth, tall, width = staged.shape
    smem = pl.BlockSpec(memory_space=pltpu.SMEM)
    vmem = pl.BlockSpec(memory_space=pltpu.VMEM)
    hbm = pl.BlockSpec(memory_space=pl.ANY)
    unit = (tall, width)
    entry = (8, key.shape[-1])
    dma = pltpu.SemaphoreType.DMA
    return pl.pallas_call(
        functools.partial(route_kernel, rounds, members, groups),
        out_shape=(
            jax.ShapeDtypeStruct((depth, layers) + unit, staged.dtype),
            jax.ShapeDtypeStruct(entry, jnp.float32),
            jax.ShapeDtypeStruct(query.shape, query.dtype),
        ),
        in_specs=[smem, smem, vmem, smem] + [vmem] * 5 + [hbm, hbm],
        out_specs=(hbm, vmem, vmem),
        scratch_shapes=[
            pltpu.VMEM((2 * depth + 3 * RMAX + 1,) + unit, staged.dtype),
            pltpu.VMEM((3, LAG) + unit, staged.dtype),
            pltpu.VMEM((3, 2 * LAG) + unit, staged.dtype),
            pltpu.VMEM((depth,) + unit, staged.dtype),
            pltpu.VMEM((depth,) + unit, staged.dtype),
            pltpu.VMEM(cache.shape, cache.dtype),
            pltpu.VMEM(cache.shape, cache.dtype),
            pltpu.VMEM((depth, key.shape[-1]), jnp.float32),
            pltpu.VMEM((members,) + entry, jnp.float32),
            pltpu.VMEM((members,) + entry, jnp.float32),
            pltpu.VMEM((groups,) + entry, jnp.float32),
            dma((2 + 3 * PIECES,)),
            dma((depth // BATCH,)),
            dma((depth // BATCH,)),
            dma((2,)),
            dma((3, LAG)),
            dma((3, 2 * LAG)),
            dma((members,)),
            dma((members,)),
            dma((groups,)),
            dma((groups,)),
        ],
        compiler_params=pltpu.CompilerParams(
            collective_id=index, has_side_effects=True, vmem_limit_bytes=VMEM_LIMIT
        ),
        name="route_%d" % rounds,
    )(*operands)


def relay(staged, source, target, members):
    place = lax.axis_index("inst")
    request_ids = jnp.arange(source.shape[0], dtype=jnp.int32)
    incoming = jnp.sum(jnp.where(target == place, request_ids, 0))
    blocks = jnp.swapaxes(staged, 0, 1)
    depth = blocks.shape[0]
    sender = source[incoming]
    share = depth // members
    relays = jnp.arange(members, dtype=jnp.int32)
    grouped = blocks.reshape((members, share) + blocks.shape[1:])
    outgoing = grouped[(relays - place) % members]
    source_of = jnp.sum(
        jnp.where(target[None, :] == relays[:, None], source[None, :], 0), axis=1
    )
    gather_back = (sender + relays) % members
    sectioned = lax.all_to_all(outgoing, "inst", split_axis=0, concat_axis=0, tiled=True)
    landed = lax.all_to_all(sectioned[source_of], "inst", split_axis=0, concat_axis=0, tiled=True)
    return landed[gather_back].reshape(blocks.shape)


def decode_attention(queries, cache_keys, cache_values, new_keys, new_values):
    layers, steps, requests, qwidth = queries.shape
    context = cache_keys.shape[2]
    kwidth = cache_keys.shape[3]
    heads_local = kwidth // HD
    grouping = qwidth // kwidth
    query = queries.reshape(layers, steps, requests, heads_local, grouping, HD)
    keyed = cache_keys.reshape(layers, requests, context, heads_local, HD)
    valued = cache_values.reshape(layers, requests, context, heads_local, HD)
    fresh_keys = new_keys.reshape(layers, steps, requests, heads_local, HD)
    fresh_values = new_values.reshape(layers, steps, requests, heads_local, HD)
    factor = 1.0 / math.sqrt(HD)
    old_scores = (
        jnp.einsum("lsrkgd,lrckd->lsrkgc", query, keyed, preferred_element_type=jnp.float32)
        * factor
    )
    new_scores = (
        jnp.einsum("lsrkgd,ltrkd->lsrkgt", query, fresh_keys, preferred_element_type=jnp.float32)
        * factor
    )
    order = jnp.arange(steps)
    visible = (order[None, :] <= order[:, None])[None, :, None, None, None, :]
    new_scores = jnp.where(visible, new_scores, -1e30)
    highest = jnp.maximum(
        jnp.max(old_scores, axis=-1, keepdims=True), jnp.max(new_scores, axis=-1, keepdims=True)
    )
    old_exp = jnp.exp(old_scores - highest)
    new_exp = jnp.where(visible, jnp.exp(new_scores - highest), 0.0)
    denominator = jnp.sum(old_exp, axis=-1, keepdims=True) + jnp.sum(
        new_exp, axis=-1, keepdims=True
    )
    old_weights = (old_exp / denominator).astype(jnp.bfloat16)
    new_weights = (new_exp / denominator).astype(jnp.bfloat16)
    mixed = jnp.einsum(
        "lsrkgc,lrckd->lsrkgd", old_weights, valued, preferred_element_type=jnp.float32
    )
    mixed = mixed + jnp.einsum(
        "lsrkgt,ltrkd->lsrkgd", new_weights, fresh_values, preferred_element_type=jnp.float32
    )
    return mixed.astype(jnp.bfloat16).reshape(layers, steps, requests, qwidth)


def local(
    queries,
    cache_keys,
    cache_values,
    new_keys,
    new_values,
    kv_pool,
    mig_lengths,
    mig_source,
    mig_target,
    block_lists,
    owner_map,
    check_key,
):
    members = lax.axis_size("inst")
    groups = lax.axis_size("tp")
    place = lax.axis_index("inst")
    pool_blocks, layers, kinds, span, width = kv_pool.shape
    pool = kv_pool.reshape(pool_blocks, layers, kinds * span, width)
    table, info, staged = plan(
        mig_lengths, mig_source, mig_target, block_lists, pool, members
    )
    layers, steps, requests, qwidth = queries.shape
    context = cache_keys.shape[2]
    heads = width // HD
    grouping = qwidth // width
    items = layers * requests
    lines = steps * grouping
    query = queries.reshape(layers, steps, requests, heads, grouping, HD)
    query = jnp.transpose(query, (0, 2, 3, 1, 4, 5)).reshape(items, heads, lines, HD)

    def pad(new):
        new = jnp.swapaxes(new, 1, 2).reshape(items, steps, width)
        return jnp.pad(new, ((0, 0), (0, 16 - steps), (0, 0)))

    operands = (
        table,
        info,
        staged,
        mig_source,
        owner_map,
        check_key,
        query,
        pad(new_keys),
        pad(new_values),
        cache_keys.reshape(items, context, width),
        cache_values.reshape(items, context, width),
    )

    def direct(index, rounds):
        return lambda operands: route(index, rounds, members, groups, operands)

    def indirect(operands):
        staged = operands[2]
        depth = staged.shape[1]
        grid = staged.reshape(layers, depth, kinds, span, heads, HD)
        projection = check_key.reshape(layers, kinds, heads, HD, -1)
        projected = jnp.einsum(
            "lbktgd,lkgde->blktge", grid, projection, preferred_element_type=jnp.float32
        )
        digest = jnp.sum(jnp.tanh(projected), axis=(1, 2, 3, 4)) / 16.0
        request_ids = jnp.arange(mig_source.shape[0], dtype=jnp.int32)
        own_request = jnp.sum(jnp.where(mig_source == place, request_ids, 0))
        owners = owner_map[own_request]
        rows = (owners // SLOTS) * 8 + owners % SLOTS
        one_hot = (rows[None, :] == jnp.arange(8 * members)[:, None]).astype(jnp.float32)
        terms = jnp.dot(
            one_hot, digest, precision=lax.Precision.HIGHEST, preferred_element_type=jnp.float32
        ).reshape(members, 8, digest.shape[-1])
        summed = lax.psum(terms, "tp")
        sums = lax.psum_scatter(summed, "inst", scatter_dimension=0, tiled=True)
        attention = decode_attention(queries, cache_keys, cache_values, new_keys, new_values)
        attention = attention.reshape(layers, steps, requests, heads, grouping, HD)
        attention = jnp.transpose(attention, (0, 2, 3, 1, 4, 5)).reshape(query.shape)
        moved = relay(staged, mig_source, mig_target, members)
        return moved, sums.reshape(terms.shape[1:]), attention

    branches = [direct(index, rounds) for index, rounds in enumerate(ROUNDS)] + [indirect]
    arrived, sums, mixed = lax.switch(info[4], branches, operands)
    arrived = arrived.reshape((arrived.shape[0],) + kv_pool.shape[1:])
    mixed = mixed.reshape(layers, requests, heads, steps, grouping, HD)
    attention = jnp.transpose(mixed, (0, 3, 1, 2, 4, 5)).reshape(queries.shape)
    return (attention, arrived, sums[:SLOTS])


def solution(mesh):
    placed = (
        P(None, None, "inst", "tp"),
        P(None, "inst", None, "tp"),
        P(None, "inst", None, "tp"),
        P(None, None, "inst", "tp"),
        P(None, None, "inst", "tp"),
        P("inst", None, None, None, "tp"),
        P(),
        P(),
        P(),
        P(),
        P(),
        P(None, None, "tp", None),
    )
    return jax.shard_map(
        local,
        mesh=mesh,
        in_specs=placed,
        out_specs=(P(None, None, "inst", "tp"), P("inst", None, None, None, "tp"), P("inst", None)),
        check_vma=False,
    )
```
